32 devices in a mesh: groups: 2 (over y), adapt: 16 (over z, x, core).
Axes of the slice: x: 2, y: 2, z: 4, core: 2. Of those that a mesh axis runs over, the one named last changes fastest.
Arguments:
- tokens: bfloat16 [256, 8192], P(('groups', 'adapt')), parts along dimension 0, may hold values from -6 to 6
- up_weight: bfloat16 [8192, 28672], P(None, 'adapt'), may hold values from -0.0625 to 0.0625
- adapter_down_weight: bfloat16 [16, 8192, 64], P('adapt'), may hold values from -0.0625 to 0.0625
- adapter_up_weight: bfloat16 [16, 64, 28672], P('adapt'), may hold values from -0.75 to 0.75
- adapter_scale_values: float32 [16], P('adapt'), may hold values from 0.25 to 2
- row_adapter_index: int32 [256, 1], P('groups'), parts along dimension 0, may hold values from 0 to 15; in each aligned block of 128 rows (0 to 127, 128 to 255, ...) at most 16 rows name the same one
Outputs:
- up_out: bfloat16 [256, 28672], P('groups', 'adapt'), parts along dimension 0
The draws below stay inside these ranges and needn't reach their ends.
There are 2 independent parts, one for each index of `groups`. The reference program is written for one: setup_inputs(seed, part) draws one part's arguments, and reference() takes and returns one part's arrays. A program takes and returns all parts, laid end to end along the dimension named above; an argument that names none is the same for every part. Nothing has to cross between parts.
Inputs may be any that keep to these rules, and one draw needn't show every extreme that they name: `row_adapter_index`: every adapter is named by at least one row and at most 16 rows; some adapter by exactly 16.
All inputs are finite; a program needn't handle non-finite values.
Results may differ from the reference program's by a relative error of at most 0.0052.
Values may be sent and summed in bfloat16 or wider, within the bound.
No kernel may reach another device: no remote copies, remote signals or barrier semaphores. Data moves between devices by JAX's collectives and lax.ppermute only.
A program may use at most 128 MiB of HBM per device.

```python
import math
import jax
import jax.numpy as jnp
import numpy as np
from jax import lax

MODEL_WIDTH = 8192
HIDDEN_WIDTH = 28672
ADAPTER_RANK = 64
CAP = 16
ROWS = 128
ADAPTER_TOTAL = 16


def level_of(own_key, extent, pieces, low, high):
    factor_of, own = 1.0, jax.random.fold_in(own_key, 6)
    for dim, parts in pieces:
        heights = jnp.exp(jax.random.uniform(jax.random.fold_in(own, dim), (parts,), jnp.float32, low / len(pieces), high / len(pieces)))
        factor_of = factor_of * jnp.repeat(heights, extent[dim] // parts).reshape([-1 if axis == dim else 1 for axis in range(len(extent))])
    return factor_of


def deal_out(rng, own, number, rows, number_of, top, most, slope):
    sequence = jax.random.permutation(rng, number_of)
    heavy_load, common = portions_of(number_of, rows * top, most, slope, True), portions_of(number_of, rows * top, most, slope, False)
    places = jnp.arange(number_of)

    def named(lengths, offset_by):
        used = int((lengths > 0).sum())
        fixed = max(1, used // 4)
        passed = fixed + (places - fixed + offset_by * (used - fixed)) % max(1, number_of - fixed)
        return jnp.zeros((number_of,), jnp.int32).at[sequence[jnp.where(places < fixed, places, passed)]].set(jnp.asarray(lengths, jnp.int32))

    lengths = jnp.where(number % 4 == 0, named(heavy_load, number // 4), named(common, number - number // 4 - 1))
    mixed = jax.random.permutation(jax.random.fold_in(own, 3), number_of)
    source_of, receiver = mixed[0:number_of // 2 * 2:2], mixed[1:number_of // 2 * 2:2]
    room = jnp.minimum(lengths[source_of] - 1, most - lengths[receiver]) // 2
    room = jnp.where((source_of == sequence[0]) | (receiver == sequence[0]) | (lengths[receiver] == 0), 0, jnp.maximum(room, 0))
    passed = jax.random.randint(jax.random.fold_in(own, 4), (number_of // 2,), 0, 1 << 20) % (room + 1)
    lengths = lengths.at[source_of].add(-passed).at[receiver].add(passed)
    members = jnp.searchsorted(jnp.cumsum(lengths), jnp.arange(rows * top), side="right").astype(jnp.int32)
    table = members.reshape(top, rows).T
    table = table[jax.random.permutation(jax.random.fold_in(own, 1), rows)]
    offset_by = jax.random.randint(jax.random.fold_in(own, 2), (rows, 1), 0, top)
    return jnp.take_along_axis(table, (jnp.arange(top)[None, :] + offset_by) % top, axis=1)


def portions_of(count, total, limit, skew, full):
    loads = [(1 << 20) // math.isqrt(standing ** skew) + 1 for standing in range(1, count + 1)]
    largest = limit if full else min(limit, max(-(-total // count), total * loads[0] // sum(loads)))
    least = 1 if total - largest >= count - 1 else 0
    holding, spare = [largest] + [least] * (count - 1), total - largest - least * (count - 1)
    while spare > 0:
        free = [i for i in range(1, count) if holding[i] < largest] or [i for i in range(1, count) if holding[i] < limit]
        mass, remaining = sum([loads[i] for i in free]), spare
        for i in free:
            more = min(limit - holding[i], max(1, remaining * loads[i] // mass), spare)
            holding[i] = holding[i] + more
            spare = spare - more
    return np.array(holding)


def bell_draw(stream_key, dims, deviation, limit, split=(), held_as=jnp.bfloat16):
    level = level_of(stream_key, dims, split, -0.22, 0.18) if split else 1.0
    result = jax.random.normal(stream_key, dims, jnp.float32) * deviation * level
    return jnp.minimum(jnp.maximum(result, -limit), limit).astype(held_as)


def setup_inputs(seed: int = 0, part: int = 0) -> dict:
    key_of = jax.random.split(jax.random.key(seed), 7)
    part_keys = jax.random.split(jax.random.fold_in(key_of[6], part), 7)
    tokens = bell_draw(part_keys[0], (ROWS, MODEL_WIDTH), 1.0, 6.0, ((0, 16),))
    up_weight = bell_draw(key_of[1], (MODEL_WIDTH, HIDDEN_WIDTH), MODEL_WIDTH ** -0.5, 0.0625, ((1, 16),))
    adapter_down_weight = bell_draw(key_of[2], (ADAPTER_TOTAL, MODEL_WIDTH, ADAPTER_RANK), MODEL_WIDTH ** -0.5, 0.0625, ((0, 16),))
    adapter_up_weight = bell_draw(key_of[3], (ADAPTER_TOTAL, ADAPTER_RANK, HIDDEN_WIDTH), ADAPTER_RANK ** -0.5, 0.75, ((0, 16),))
    adapter_scale_values = jnp.clip(jnp.exp(math.log(2.0) - 2.0794415 * jax.random.uniform(key_of[4], (ADAPTER_TOTAL,), jnp.float32) ** level_of(key_of[4], (ADAPTER_TOTAL,), ((0, 16),), -0.2, 0.2)), 0.25, 2.0)
    row_adapter_index_keys = jax.random.split(jax.random.fold_in(part_keys[5], 1), ROWS // ROWS)
    row_adapter_index_turns = jax.random.permutation(jax.random.fold_in(part_keys[5], 3), ROWS // ROWS)
    row_adapter_index = jax.vmap(lambda own, number: deal_out(jax.random.fold_in(part_keys[5], 2), own, number, ROWS, ADAPTER_TOTAL, 1, CAP, 2))(row_adapter_index_keys, row_adapter_index_turns).reshape((ROWS, 1))
    return {"tokens": tokens, "up_weight": up_weight, "adapter_down_weight": adapter_down_weight, "adapter_up_weight": adapter_up_weight, "adapter_scale_values": adapter_scale_values, "row_adapter_index": row_adapter_index}


def reference(tokens, up_weight, adapter_down_weight, adapter_up_weight, adapter_scale_values, row_adapter_index):
    row_ids = row_adapter_index[:, 0].astype(jnp.int32)
    base_part = jnp.dot(tokens, up_weight, preferred_element_type=jnp.float32)
    block_count = row_ids.shape[0] // 16

    def one_block(block_index):
        start = (block_index * 16).astype(jnp.int32)
        input_rows = lax.dynamic_slice_in_dim(tokens, start, 16, 0).astype(jnp.float32)
        selected_adapter = lax.dynamic_slice_in_dim(row_ids, start, 16, 0)
        rank_output = jnp.einsum("vj,vjm->vm", input_rows, adapter_down_weight[selected_adapter].astype(jnp.float32))
        adapter_scale = (rank_output * adapter_scale_values[selected_adapter][:, None]).astype(jnp.bfloat16)
        widened_output = jnp.einsum("io,ion->in", adapter_scale.astype(jnp.float32), adapter_up_weight[selected_adapter].astype(jnp.float32))
        return widened_output.astype(jnp.bfloat16)

    deltas = lax.map(one_block, jnp.arange(block_count, dtype=jnp.int32))
    deltas = deltas.reshape(row_ids.shape[0], -1)
    return (base_part + deltas.astype(jnp.float32)).astype(jnp.bfloat16)
```

```python
import functools

import jax
import jax.numpy as jnp
from jax import lax
from jax.experimental import pallas as pl
from jax.experimental.pallas import tpu as pltpu
from jax.sharding import PartitionSpec as P

CAP = 16
AXIS = "adapt"
MIB = 1 << 20


def swap(x, mask, count):
    return lax.ppermute(x, AXIS, [(i, i ^ mask) for i in range(count)])


def gather_chunks(x, count):
    near = min(4, count)
    chunks = {0: x}
    for far in range(near, count, near):
        chunks[far] = swap(x, far, count)
    for mask in (2, 1):
        if mask < near:
            for key in sorted(chunks):
                chunks[key ^ mask] = swap(chunks[key], mask, count)
    return [chunks[m] for m in range(count)]


def delta_kernel(scale_ref, owned_ref, ids_ref, rank_ref, x_ref, down_ref, up_ref, out_ref):
    low = lax.dot_general(
        x_ref[...], down_ref[...], (((1,), (1,)), ((), ())), preferred_element_type=jnp.float32
    )
    low = (low * scale_ref[0]).astype(jnp.bfloat16)
    slots = lax.broadcasted_iota(jnp.int32, (CAP, low.shape[0]), 0)
    pick = (ids_ref[...] == owned_ref[0]) & (rank_ref[...] == slots)
    pick = jnp.where(pick, 1.0, 0.0).astype(jnp.bfloat16)
    low = jnp.dot(pick, low, preferred_element_type=jnp.float32).astype(jnp.bfloat16)
    width = out_ref.shape[2]
    for j in range(out_ref.shape[0]):
        out_ref[j] = jnp.dot(
            low, up_ref[:, j * width : (j + 1) * width], preferred_element_type=jnp.float32
        ).astype(jnp.bfloat16)


def make_delta(x, down, up, scale, owned, ids, rank, count):
    hidden = up.shape[1]
    width = hidden // count
    vmem = pl.BlockSpec(memory_space=pltpu.VMEM)
    smem = pl.BlockSpec(memory_space=pltpu.SMEM)
    out = jax.ShapeDtypeStruct((count, CAP, width), jnp.bfloat16)
    if width % 128:
        low = (jnp.dot(x, down.T, preferred_element_type=jnp.float32) * scale[0]).astype(jnp.bfloat16)
        pick = (ids == owned[0]) & (rank == jnp.arange(CAP, dtype=jnp.int32)[:, None])
        low = jnp.dot(pick.astype(jnp.bfloat16), low, preferred_element_type=jnp.float32)
        delta = jnp.dot(low.astype(jnp.bfloat16), up, preferred_element_type=jnp.float32)
        return delta.astype(jnp.bfloat16).reshape(CAP, count, width).transpose(1, 0, 2)
    return pl.pallas_call(
        delta_kernel,
        out_shape=out,
        in_specs=[smem, smem, vmem, vmem, vmem, vmem, vmem],
        out_specs=vmem,
        compiler_params=pltpu.CompilerParams(vmem_limit_bytes=24 * MIB),
        cost_estimate=pl.CostEstimate(
            flops=2 * x.size * 64, bytes_accessed=2 * (x.size + down.size + up.size), transcendentals=0
        ),
    )(scale, owned, ids, rank, x, down, up)


def combine_kernel(rows_each, me_ref, slot_ref, base_ref, arrived_ref, out_ref, acc):
    rows = base_ref.shape[0]
    for m in range(rows // rows_each):
        at = pl.multiple_of((me_ref[0] ^ m) * rows_each, rows_each)
        acc[pl.ds(at, rows_each), :] = base_ref[m * rows_each : (m + 1) * rows_each, :]
    places = lax.broadcasted_iota(jnp.int32, (rows, arrived_ref.shape[0]), 1)
    pick = jnp.where(slot_ref[...] == places, 1.0, 0.0).astype(jnp.bfloat16)
    delta = jnp.dot(pick, arrived_ref[...], preferred_element_type=jnp.float32)
    out_ref[...] = (acc[...] + delta).astype(jnp.bfloat16)


def combine(base, arrived, slot, me, rows_each):
    rows, width = base.shape
    vmem = pl.BlockSpec(memory_space=pltpu.VMEM)
    smem = pl.BlockSpec(memory_space=pltpu.SMEM)
    return pl.pallas_call(
        functools.partial(combine_kernel, rows_each),
        out_shape=jax.ShapeDtypeStruct((rows, width), jnp.bfloat16),
        in_specs=[smem, vmem, vmem, vmem],
        out_specs=vmem,
        scratch_shapes=[pltpu.VMEM((rows, width), jnp.float32)],
        compiler_params=pltpu.CompilerParams(vmem_limit_bytes=24 * MIB),
        cost_estimate=pl.CostEstimate(
            flops=2 * rows * arrived.size, bytes_accessed=4 * base.size, transcendentals=0
        ),
    )(me, slot, base, arrived)


def body(count, tokens, up_weight, down, up, scale, row_index):
    me = lax.axis_index(AXIS)
    rows_each = tokens.shape[0]
    ids = row_index[:, 0]
    rows = ids.shape[0]
    adapters = down.shape[0] * count
    matches = (ids[:, None] == jnp.arange(adapters, dtype=jnp.int32)[None, :]).astype(jnp.int32)
    running = jnp.cumsum(matches, axis=0)
    rank = jnp.sum(matches * running, axis=1) - 1
    slot = (ids * CAP + rank)[:, None]
    place = jnp.arange(rows, dtype=jnp.int32)
    place = ((place // rows_each) ^ me) * rows_each + place % rows_each
    ids_here, rank_here = ids[place], rank[place]
    me = me.astype(jnp.int32)[None]

    x = jnp.concatenate(gather_chunks(tokens, count), axis=0)
    delta = make_delta(
        x,
        jnp.swapaxes(down[0], 0, 1),
        up[0],
        scale,
        me,
        ids_here[None, :],
        rank_here[None, :],
        count,
    )
    arrived = lax.all_to_all(delta, AXIS, split_axis=0, concat_axis=0, tiled=True)
    base = jnp.dot(x, up_weight, preferred_element_type=jnp.float32)
    return combine(base, arrived.reshape(count * CAP, -1), slot, me, rows_each)


def solution(mesh):
    placed = (
        P(("groups", AXIS), None),
        P(None, AXIS),
        P(AXIS, None, None),
        P(AXIS, None, None),
        P(AXIS),
        P("groups", None),
    )
    return jax.shard_map(
        functools.partial(body, mesh.shape[AXIS]),
        mesh=mesh,
        in_specs=placed,
        out_specs=P("groups", AXIS),
        check_vma=False,
    )
```

```python
import functools

import jax
import jax.numpy as jnp
from jax import lax
from jax.experimental import pallas as pl
from jax.experimental.pallas import tpu as pltpu
from jax.sharding import PartitionSpec as P

CAP = 16
AXIS = "adapt"
MIB = 1 << 20
STEP = 1024
PLAN_FLOPS = 6_000_000_000
VMEM = pl.BlockSpec(memory_space=pltpu.VMEM)
SMEM = pl.BlockSpec(memory_space=pltpu.SMEM)
HBM = pl.BlockSpec(memory_space=pltpu.HBM)


def swap(x, mask, count):
    return lax.ppermute(x, AXIS, [(i, i ^ mask) for i in range(count)])


def after(value, *others):
    return lax.optimization_barrier((value, *others))[0]


def gather_rows(x, count, early=()):
    far, bits = count // 2, []
    beside = swap(x, 1, count)
    chunks = {0: x, far: swap(x, far, count)}
    bit = far // 2
    while bit > 1:
        chunks[bit] = swap(x, bit, count)
        bits.append(bit)
        bit //= 2
    late = after(x, beside)
    for key in range(4, far, 4):
        chunks[far ^ key] = swap(late, far ^ key, count)
        if key not in chunks:
            chunks[key] = swap(late, key, count)
    chunks[far] = after(chunks[far], *early)
    for key in sorted(chunks):
        if key ^ 2 not in chunks:
            chunks[key ^ 2] = swap(chunks[key], 2, count)
    for key in sorted(chunks):
        chunks[key ^ 1] = swap(chunks[key], 1, count) if key else beside
    return [chunks[m] for m in range(count)]


def iota(shape, dim):
    return lax.broadcasted_iota(jnp.int32, shape, dim)


def one_hot(condition):
    return jnp.where(condition, 1.0, 0.0).astype(jnp.bfloat16)


def product(a, b):
    return jnp.dot(a, b, preferred_element_type=jnp.float32)


def ranks(ids, adapters):
    rows = ids.shape[1]
    matches = ids == iota((adapters, rows), 0)
    earlier = one_hot(iota((rows, rows), 0) < iota((rows, rows), 1))
    before = product(one_hot(matches), earlier)
    return jnp.sum(jnp.where(matches, before, 0.0), axis=0, keepdims=True).astype(jnp.int32)


def origins(me, adapters, rows):
    place = iota((1, rows), 1)
    each = rows // adapters
    return ((place // each) ^ me) * each + place % each


def picks_of(ids, me, owned, adapters):
    rows = ids.shape[1]
    pick = one_hot((ids == owned) & (ranks(ids, adapters) == iota((CAP, rows), 0)))
    back = one_hot(iota((rows, rows), 0) == origins(me, adapters, rows))
    return product(pick, back).astype(jnp.bfloat16)


def places_of(ids, adapters, slots):
    rows = ids.shape[1]
    return one_hot(ids * CAP + ranks(ids, adapters) == iota((slots, rows), 0))


def plan_kernel(count, me_ref, ids_ref, down_ref, pick_ref, turned_ref):
    pick_ref[...] = picks_of(ids_ref[...], me_ref[0], me_ref[0], count)
    turned_ref[...] = down_ref[...].T


def make_plan(ids, down, me, count):
    rows = ids.shape[1]
    return pl.pallas_call(
        functools.partial(plan_kernel, count),
        out_shape=(
            jax.ShapeDtypeStruct((CAP, rows), jnp.bfloat16),
            jax.ShapeDtypeStruct(down.shape[::-1], jnp.bfloat16),
        ),
        in_specs=[SMEM, VMEM, VMEM],
        out_specs=(VMEM, VMEM),
        compiler_params=pltpu.CompilerParams(vmem_limit_bytes=24 * MIB),
        cost_estimate=pl.CostEstimate(flops=PLAN_FLOPS, bytes_accessed=MIB, transcendentals=0),
        name="plan",
    )(me, ids, down)


def join(pairs, chunk_refs, x_ref):
    each = chunk_refs[0].shape[0]
    for i, pair in enumerate(pairs):
        both = jnp.concatenate([chunk_refs[2 * i][...], chunk_refs[2 * i + 1][...]], axis=0)
        x_ref[pair * 2 * each : (pair + 1) * 2 * each, :] = both


def late_rows(rest_hbm, x_ref, sem, inward):
    copies = []
    for i in range(sem.shape[0]):
        each = rest_hbm.shape[0] // sem.shape[0]
        outer = rest_hbm.at[pl.ds(i * each, each)]
        inner = x_ref.at[pl.ds((2 * i + 1) * each, each)]
        ends = (outer, inner) if inward else (inner, outer)
        copies.append(pltpu.make_async_copy(*ends, sem.at[i]))
        copies[-1].start()
    return copies


def delta_kernel(scale_ref, pick_ref, down_ref, up_ref, *refs):
    chunk_refs, (out_hbm, rest_hbm, x_ref, out_ref, sem, rest_sem) = refs[:-6], refs[-6:]
    count, _, width = out_ref.shape
    join(range(count // 2), chunk_refs, x_ref)
    copies = late_rows(rest_hbm, x_ref, rest_sem, False)
    low = (product(x_ref[...], down_ref[...]) * scale_ref[0]).astype(jnp.bfloat16)
    low = product(pick_ref[...], low).astype(jnp.bfloat16)
    for j in range(count):
        out_ref[j] = product(low, up_ref[:, j * width : (j + 1) * width]).astype(jnp.bfloat16)
        if j % 4 == 3:
            part = pl.ds(j - 3, 4)
            copies.append(pltpu.make_async_copy(out_ref.at[part], out_hbm.at[part], sem.at[j // 4]))
            copies[-1].start()
    for copy in copies:
        copy.wait()


def make_deltas(chunks, down, up, scale, pick):
    count = len(chunks)
    width = up.shape[1] // count
    each, depth = chunks[0].shape
    rows = count * each
    return pl.pallas_call(
        delta_kernel,
        out_shape=(
            pltpu.HBM((count, CAP, width), jnp.bfloat16),
            pltpu.HBM((rows // 2, depth), jnp.bfloat16),
        ),
        in_specs=[SMEM] + [VMEM] * (count + 3),
        out_specs=(HBM, HBM),
        scratch_shapes=[
            pltpu.VMEM((rows, depth), jnp.bfloat16),
            pltpu.VMEM((count, CAP, width), jnp.bfloat16),
            pltpu.SemaphoreType.DMA((count // 4,)),
            pltpu.SemaphoreType.DMA((count // 4,)),
        ],
        compiler_params=pltpu.CompilerParams(vmem_limit_bytes=24 * MIB),
        cost_estimate=pl.CostEstimate(
            flops=2 * depth * rows * 64,
            bytes_accessed=2 * (depth * rows + down.size + up.size),
            transcendentals=0,
        ),
        name="corrections",
    )(scale, pick, down, up, *chunks)


def base_kernel(weight_ref, rest_hbm, *refs):
    chunk_refs, (out_ref, x_ref, sem) = refs[:-3], refs[-3:]
    depth, width = weight_ref.shape
    size = min(STEP, depth)
    copies = late_rows(rest_hbm, x_ref, sem, True)
    join(range(0, len(chunk_refs), 2), chunk_refs, x_ref)
    out_ref[...] = jnp.zeros_like(out_ref)
    for copy in copies:
        copy.wait()

    def step(index, block_ref):
        columns = pl.ds(pl.multiple_of(index.index[0] * size, size), size)
        out_ref[...] += product(x_ref[:, columns], block_ref[...])

    pltpu.emit_pipeline(
        step,
        grid=(depth // size,),
        in_specs=[pl.BlockSpec((size, width), lambda k: (k, 0), pipeline_mode=pl.Buffered(3))],
        _explicit_indices=True,
    )(weight_ref)


def base_product(chunks, rest, weight):
    depth, width = weight.shape
    count = len(chunks)
    rows = count * chunks[0].shape[0]
    early = [chunk for m, chunk in enumerate(chunks) if not m & 2]
    return pl.pallas_call(
        base_kernel,
        out_shape=jax.ShapeDtypeStruct((rows, width), jnp.float32),
        in_specs=[HBM, HBM] + [VMEM] * len(early),
        out_specs=VMEM,
        scratch_shapes=[pltpu.VMEM((rows, depth), jnp.bfloat16), pltpu.SemaphoreType.DMA((count // 4,))],
        compiler_params=pltpu.CompilerParams(vmem_limit_bytes=24 * MIB),
        cost_estimate=pl.CostEstimate(
            flops=2 * rows * depth * width, bytes_accessed=2 * weight.size, transcendentals=0
        ),
        name="base",
    )(weight, rest, *early)


def combine_kernel(me_ref, ids_ref, base_ref, arrived_ref, out_ref, acc):
    rows = acc.shape[0]
    count = arrived_ref.shape[0] // CAP
    each = rows // count
    for m in range(count):
        at = pl.multiple_of((me_ref[0] ^ m) * each, each)
        acc[pl.ds(at, each), :] = base_ref[m * each : (m + 1) * each, :]
    pick = places_of(ids_ref[...], count, arrived_ref.shape[0])
    delta = lax.dot_general(
        pick, arrived_ref[...], (((0,), (0,)), ((), ())), preferred_element_type=jnp.float32
    )
    out_ref[...] = (acc[...] + delta).astype(jnp.bfloat16)


def combine(base, arrived, ids, me):
    rows, width = base.shape
    return pl.pallas_call(
        combine_kernel,
        out_shape=jax.ShapeDtypeStruct((rows, width), jnp.bfloat16),
        in_specs=[SMEM] + [VMEM] * 3,
        out_specs=VMEM,
        scratch_shapes=[pltpu.VMEM((rows, width), jnp.float32)],
        compiler_params=pltpu.CompilerParams(vmem_limit_bytes=24 * MIB),
        cost_estimate=pl.CostEstimate(
            flops=2 * rows * arrived.size, bytes_accessed=4 * base.size, transcendentals=0
        ),
        name="combine",
    )(me, ids, base, arrived)


def plain_body(chunks, up_weight, down, up, scale, ids, me):
    count = len(chunks)
    rows, width = ids.shape[1], up_weight.shape[1]
    x = jnp.concatenate(chunks, axis=0)
    low = lax.dot_general(x, down, (((1,), (1,)), ((), ())), preferred_element_type=jnp.float32)
    pick = picks_of(ids, me[0], me[0], count)
    low = product(pick, (low * scale[0]).astype(jnp.bfloat16)).astype(jnp.bfloat16)
    delta = product(low, up).astype(jnp.bfloat16).reshape(CAP, count, width)
    arrived = lax.all_to_all(delta, AXIS, split_axis=1, concat_axis=0, tiled=True)
    base = product(x, up_weight)[origins(me[0], count, rows)[0]]
    slot = (ids * CAP + ranks(ids, count))[0]
    return (base + arrived.reshape(count * CAP, width)[slot].astype(jnp.float32)).astype(jnp.bfloat16)


def body(count, tokens, up_weight, down, up, scale, row_index):
    me = lax.axis_index(AXIS).astype(jnp.int32)[None]
    ids = row_index.reshape(1, -1)
    down, up = jnp.swapaxes(down[0], 0, 1), up[0]
    if up_weight.shape[1] % 128:
        chunks = gather_rows(tokens, count)
        return plain_body(chunks, up_weight, down, up, scale, ids, me)
    pick, down = make_plan(ids, down, me, count)
    chunks = gather_rows(tokens, count, (pick,))
    delta, rest = make_deltas(chunks, down, up, scale, pick)
    arrived = lax.all_to_all(delta, AXIS, split_axis=0, concat_axis=0, tiled=True)
    base = base_product(chunks, rest, up_weight)
    return combine(base, arrived.reshape(count * CAP, -1), ids, me)


def solution(mesh):
    placed = (
        P(("groups", AXIS), None),
        P(None, AXIS),
        P(AXIS, None, None),
        P(AXIS, None, None),
        P(AXIS),
        P("groups", None),
    )
    return jax.shard_map(
        functools.partial(body, mesh.shape[AXIS]),
        mesh=mesh,
        in_specs=placed,
        out_specs=P("groups", AXIS),
        check_vma=False,
    )
```

```python
import functools

import jax
import jax.numpy as jnp
from jax import lax
from jax.experimental import pallas as pl
from jax.experimental.pallas import tpu as pltpu
from jax.sharding import PartitionSpec as P

CAP = 16
AXIS = "adapt"
MIB = 1 << 20
STEP = 1024
PLAN_FLOPS = 6_000_000_000
VMEM = pl.BlockSpec(memory_space=pltpu.VMEM)
SMEM = pl.BlockSpec(memory_space=pltpu.SMEM)
HBM = pl.BlockSpec(memory_space=pltpu.HBM)


def swap(x, mask, count):
    return lax.ppermute(x, AXIS, [(i, i ^ mask) for i in range(count)])


def after(value, *others):
    return lax.optimization_barrier((value, *others))[0]


def gather_rows(x, count, early=()):
    far, bits = count // 2, []
    beside = swap(x, 1, count)
    chunks = {0: x, far: swap(x, far, count)}
    bit = far // 2
    while bit > 1:
        chunks[bit] = swap(x, bit, count)
        bits.append(bit)
        bit //= 2
    late = after(x, beside)
    for key in range(4, far, 4):
        chunks[far ^ key] = swap(late, far ^ key, count)
        if key not in chunks:
            chunks[key] = swap(late, key, count)
    chunks[far] = after(chunks[far], *early)
    for key in sorted(chunks):
        if key ^ 2 not in chunks:
            chunks[key ^ 2] = swap(chunks[key], 2, count)
    for key in sorted(chunks):
        chunks[key ^ 1] = swap(chunks[key], 1, count) if key else beside
    return [chunks[m] for m in range(count)]


def start_order(chips):
    near, far = list(range(1, chips // 2)), list(range(chips // 2, chips))
    return near[:2] + far + near[2:]


def iota(shape, dim):
    return lax.broadcasted_iota(jnp.int32, shape, dim)


def one_hot(condition):
    return jnp.where(condition, 1.0, 0.0).astype(jnp.bfloat16)


def product(a, b):
    return jnp.dot(a, b, preferred_element_type=jnp.float32)


def ranks(ids, adapters):
    rows = ids.shape[1]
    matches = ids == iota((adapters, rows), 0)
    earlier = one_hot(iota((rows, rows), 0) < iota((rows, rows), 1))
    before = product(one_hot(matches), earlier)
    return jnp.sum(jnp.where(matches, before, 0.0), axis=0, keepdims=True).astype(jnp.int32)


def origins(me, adapters, rows):
    place = iota((1, rows), 1)
    each = rows // adapters
    return ((place // each) ^ me) * each + place % each


def picks_of(ids, me, owned, adapters):
    rows = ids.shape[1]
    pick = one_hot((ids == owned) & (ranks(ids, adapters) == iota((CAP, rows), 0)))
    back = one_hot(iota((rows, rows), 0) == origins(me, adapters, rows))
    return product(pick, back).astype(jnp.bfloat16)


def places_of(ids, me, adapters, slots):
    rows = ids.shape[1]
    apart = ids ^ me
    slot = ((apart & 1) * (adapters // 2) + apart // 2) * CAP + ranks(ids, adapters)
    return one_hot(slot == iota((slots, rows), 0))


def plan_kernel(count, me_ref, ids_ref, down_ref, pick_ref, turned_ref):
    pick_ref[...] = picks_of(ids_ref[...], me_ref[0], me_ref[0], count)
    turned_ref[...] = down_ref[...].T


def make_plan(ids, down, me, count):
    rows = ids.shape[1]
    return pl.pallas_call(
        functools.partial(plan_kernel, count),
        out_shape=(
            jax.ShapeDtypeStruct((CAP, rows), jnp.bfloat16),
            jax.ShapeDtypeStruct(down.shape[::-1], jnp.bfloat16),
        ),
        in_specs=[SMEM, VMEM, VMEM],
        out_specs=(VMEM, VMEM),
        compiler_params=pltpu.CompilerParams(vmem_limit_bytes=24 * MIB),
        cost_estimate=pl.CostEstimate(flops=PLAN_FLOPS, bytes_accessed=MIB, transcendentals=0),
        name="plan",
    )(me, ids, down)


def join(pairs, chunk_refs, x_ref):
    each = chunk_refs[0].shape[0]
    for i, pair in enumerate(pairs):
        both = jnp.concatenate([chunk_refs[2 * i][...], chunk_refs[2 * i + 1][...]], axis=0)
        x_ref[pair * 2 * each : (pair + 1) * 2 * each, :] = both


def delta_kernel(scale_ref, me_ref, pick_ref, down_ref, up_ref, *refs):
    chips = (len(refs) - 1) // 3
    chunk_refs, out_refs, x_ref = refs[: 2 * chips], refs[2 * chips : -1], refs[-1]
    width = out_refs[0].shape[1]
    join(range(chips), chunk_refs, x_ref)
    low = (product(x_ref[...], down_ref[...]) * scale_ref[0]).astype(jnp.bfloat16)
    low = product(pick_ref[...], low).astype(jnp.bfloat16)
    for i, ref in enumerate(out_refs):
        for core in range(2):
            device = me_ref[0] ^ (2 * i + core)
            columns = pl.ds(pl.multiple_of(device * width, 128), width)
            delta = product(low, up_ref[:, columns])
            ref[core * CAP : (core + 1) * CAP, :] = delta.astype(jnp.bfloat16)


def make_deltas(chunks, down, up, scale, pick, me):
    count = len(chunks)
    width = up.shape[1] // count
    each, depth = chunks[0].shape
    rows = count * each
    return pl.pallas_call(
        delta_kernel,
        out_shape=tuple(
            jax.ShapeDtypeStruct((2 * CAP, width), jnp.bfloat16) for _ in range(count // 2)
        )
        + (jax.ShapeDtypeStruct((rows, depth), jnp.bfloat16),),
        in_specs=[SMEM, SMEM] + [VMEM] * (count + 3),
        out_specs=(VMEM,) * (count // 2 + 1),
        compiler_params=pltpu.CompilerParams(vmem_limit_bytes=24 * MIB),
        cost_estimate=pl.CostEstimate(
            flops=2 * depth * rows * 64,
            bytes_accessed=2 * (depth * rows + down.size + up.size),
            transcendentals=0,
        ),
        name="corrections",
    )(scale, me, pick, down, up, *chunks)


def base_kernel(me_ref, ids_ref, x_ref, weight_ref, out_ref, place_ref, acc):
    depth, width = weight_ref.shape
    size = min(STEP, depth)
    rows, slots = place_ref.shape
    count = slots // CAP
    place_ref[...] = places_of(ids_ref[...], me_ref[0], count, slots).T
    acc[...] = jnp.zeros_like(acc)

    def step(index, block_ref):
        columns = pl.ds(pl.multiple_of(index.index[0] * size, size), size)
        acc[...] += product(x_ref[:, columns], block_ref[...])

    pltpu.emit_pipeline(
        step,
        grid=(depth // size,),
        in_specs=[pl.BlockSpec((size, width), lambda k: (k, 0), pipeline_mode=pl.Buffered(3))],
        _explicit_indices=True,
    )(weight_ref)
    each = rows // count
    for m in range(count):
        at = pl.multiple_of((me_ref[0] ^ m) * each, each)
        out_ref[pl.ds(at, each), :] = acc[m * each : (m + 1) * each, :]


def base_product(x, weight, ids, me, count):
    rows, depth = x.shape
    width = weight.shape[1]
    slots = count * CAP
    return pl.pallas_call(
        base_kernel,
        out_shape=(
            jax.ShapeDtypeStruct((rows, width), jnp.float32),
            jax.ShapeDtypeStruct((rows, slots), jnp.bfloat16),
        ),
        in_specs=[SMEM, VMEM, VMEM, HBM],
        out_specs=(VMEM, VMEM),
        scratch_shapes=[pltpu.VMEM((rows, width), jnp.float32)],
        compiler_params=pltpu.CompilerParams(vmem_limit_bytes=24 * MIB),
        cost_estimate=pl.CostEstimate(
            flops=2 * rows * depth * width, bytes_accessed=2 * weight.size, transcendentals=0
        ),
        name="base",
    )(me, ids, x, weight)


def combine_kernel(place_ref, base_ref, mate_ref, *refs):
    arrived_refs, (out_hbm, out_ref, slots, sem) = refs[:-4], refs[-4:]
    chips = len(arrived_refs)
    width = out_ref.shape[2]
    for i, ref in enumerate(arrived_refs):
        slots[i * CAP : (i + 1) * CAP, :] = ref[:CAP, :]
    half = chips * CAP
    slots[half:, :] = mate_ref[...]
    copies = []
    for i in range(out_ref.shape[0]):
        columns = pl.ds(i * width, width)
        delta = product(place_ref[...], slots[:, columns])
        out_ref[i] = (base_ref[:, columns] + delta).astype(jnp.bfloat16)
        copies.append(pltpu.make_async_copy(out_ref.at[i], out_hbm.at[:, columns], sem.at[i]))
        copies[-1].start()
    for copy in copies:
        copy.wait()


def combine(base, arrived, mate, place):
    rows, width = base.shape
    parts = 2 if width % 256 == 0 else 1
    return pl.pallas_call(
        combine_kernel,
        out_shape=jax.ShapeDtypeStruct((rows, width), jnp.bfloat16),
        in_specs=[VMEM] * (3 + len(arrived)),
        out_specs=HBM,
        scratch_shapes=[
            pltpu.VMEM((parts, rows, width // parts), jnp.bfloat16),
            pltpu.VMEM((place.shape[1], width), jnp.bfloat16),
            pltpu.SemaphoreType.DMA((parts,)),
        ],
        compiler_params=pltpu.CompilerParams(vmem_limit_bytes=24 * MIB),
        cost_estimate=pl.CostEstimate(
            flops=2 * rows * place.size, bytes_accessed=4 * base.size, transcendentals=0
        ),
        name="combine",
    )(place, base, mate, *arrived)


def plain_body(chunks, up_weight, down, up, scale, ids, me):
    count = len(chunks)
    rows, width = ids.shape[1], up_weight.shape[1]
    x = jnp.concatenate(chunks, axis=0)
    low = lax.dot_general(x, down, (((1,), (1,)), ((), ())), preferred_element_type=jnp.float32)
    pick = picks_of(ids, me[0], me[0], count)
    low = product(pick, (low * scale[0]).astype(jnp.bfloat16)).astype(jnp.bfloat16)
    delta = product(low, up).astype(jnp.bfloat16).reshape(CAP, count, width)
    arrived = lax.all_to_all(delta, AXIS, split_axis=1, concat_axis=0, tiled=True)
    base = product(x, up_weight)[origins(me[0], count, rows)[0]]
    slot = (ids * CAP + ranks(ids, count))[0]
    return (base + arrived.reshape(count * CAP, width)[slot].astype(jnp.float32)).astype(jnp.bfloat16)


def body(count, tokens, up_weight, down, up, scale, row_index):
    me = lax.axis_index(AXIS).astype(jnp.int32)[None]
    ids = row_index.reshape(1, -1)
    down, up = jnp.swapaxes(down[0], 0, 1), up[0]
    if up_weight.shape[1] % 128:
        chunks = gather_rows(tokens, count)
        return plain_body(chunks, up_weight, down, up, scale, ids, me)
    pick, down = make_plan(ids, down, me, count)
    chunks = gather_rows(tokens, count, (pick,))
    *deltas, x = make_deltas(chunks, down, up, scale, pick, me)
    arrived = {0: deltas[0]}
    order = start_order(count // 2)
    for i in order:
        arrived[i] = swap(deltas[i], 2 * i, count)
    base, place = base_product(x, up_weight, ids, me, count)
    *held, base = lax.optimization_barrier((*(arrived[i] for i in order), base))
    arrived.update(zip(order, held))
    arrived = [arrived[i] for i in range(count // 2)]
    mate = swap(jnp.concatenate([part[CAP:] for part in arrived], axis=0), 1, count)
    return combine(base, arrived, mate, place)


def solution(mesh):
    placed = (
        P(("groups", AXIS), None),
        P(None, AXIS),
        P(AXIS, None, None),
        P(AXIS, None, None),
        P(AXIS),
        P("groups", None),
    )
    return jax.shard_map(
        functools.partial(body, mesh.shape[AXIS]),
        mesh=mesh,
        in_specs=placed,
        out_specs=P("groups", AXIS),
        check_vma=False,
    )
```

```python
import functools

import jax
import jax.numpy as jnp
from jax import lax
from jax.experimental import pallas as pl
from jax.experimental.pallas import tpu as pltpu
from jax.sharding import PartitionSpec as P

CAP = 16
AXIS = "adapt"
MIB = 1 << 20
STEP = 1024
PLAN_FLOPS = 6_000_000_000
VMEM = pl.BlockSpec(memory_space=pltpu.VMEM)
SMEM = pl.BlockSpec(memory_space=pltpu.SMEM)
HBM = pl.BlockSpec(memory_space=pltpu.HBM)


def swap(x, mask, count):
    return lax.ppermute(x, AXIS, [(i, i ^ mask) for i in range(count)])


def after(value, *others):
    return lax.optimization_barrier((value, *others))[0]


def gather_rows(x, count, early=()):
    far, bits = count // 2, []
    beside = swap(x, 1, count)
    chunks = {0: x, far: swap(x, far, count)}
    bit = far // 2
    while bit > 1:
        chunks[bit] = swap(x, bit, count)
        bits.append(bit)
        bit //= 2
    late = after(x, beside)
    for key in range(4, far, 4):
        chunks[far ^ key] = swap(late, far ^ key, count)
        if key not in chunks:
            chunks[key] = swap(late, key, count)
    chunks[far] = after(chunks[far], *early)
    for key in sorted(chunks):
        if key ^ 2 not in chunks:
            chunks[key ^ 2] = swap(chunks[key], 2, count)
    for key in sorted(chunks):
        chunks[key ^ 1] = swap(chunks[key], 1, count) if key else beside
    return [chunks[m] for m in range(count)]


def start_order(chips):
    near, far = list(range(1, chips // 2)), list(range(chips // 2, chips))
    return near[:2] + far + near[2:]


def iota(shape, dim):
    return lax.broadcasted_iota(jnp.int32, shape, dim)


def one_hot(condition):
    return jnp.where(condition, 1.0, 0.0).astype(jnp.bfloat16)


def product(a, b):
    return jnp.dot(a, b, preferred_element_type=jnp.float32)


def ranks(ids, adapters):
    rows = ids.shape[1]
    matches = ids == iota((adapters, rows), 0)
    earlier = one_hot(iota((rows, rows), 0) < iota((rows, rows), 1))
    before = product(one_hot(matches), earlier)
    return jnp.sum(jnp.where(matches, before, 0.0), axis=0, keepdims=True).astype(jnp.int32)


def origins(me, adapters, rows):
    place = iota((1, rows), 1)
    each = rows // adapters
    return ((place // each) ^ me) * each + place % each


def picks_of(ids, me, owned, adapters):
    rows = ids.shape[1]
    pick = one_hot((ids == owned) & (ranks(ids, adapters) == iota((CAP, rows), 0)))
    back = one_hot(iota((rows, rows), 0) == origins(me, adapters, rows))
    return product(pick, back).astype(jnp.bfloat16)


def places_of(ids, me, adapters, slots):
    rows = ids.shape[1]
    apart = ids ^ me
    slot = ((apart & 1) * (adapters // 2) + apart // 2) * CAP + ranks(ids, adapters)
    return one_hot(slot == iota((slots, rows), 0))


def plan_kernel(count, me_ref, ids_ref, down_ref, pick_ref, turned_ref):
    pick_ref[...] = picks_of(ids_ref[...], me_ref[0], me_ref[0], count)
    turned_ref[...] = down_ref[...].T


def make_plan(ids, down, me, count):
    rows = ids.shape[1]
    return pl.pallas_call(
        functools.partial(plan_kernel, count),
        out_shape=(
            jax.ShapeDtypeStruct((CAP, rows), jnp.bfloat16),
            jax.ShapeDtypeStruct(down.shape[::-1], jnp.bfloat16),
        ),
        in_specs=[SMEM, VMEM, VMEM],
        out_specs=(VMEM, VMEM),
        compiler_params=pltpu.CompilerParams(vmem_limit_bytes=24 * MIB),
        cost_estimate=pl.CostEstimate(flops=PLAN_FLOPS, bytes_accessed=MIB, transcendentals=0),
        name="plan",
    )(me, ids, down)


def join(pairs, chunk_refs, x_ref):
    each = chunk_refs[0].shape[0]
    for i, pair in enumerate(pairs):
        both = jnp.concatenate([chunk_refs[2 * i][...], chunk_refs[2 * i + 1][...]], axis=0)
        x_ref[pair * 2 * each : (pair + 1) * 2 * each, :] = both


def write_deltas(low, up_ref, first_device, ref):
    width = ref.shape[1]
    for core in range(2):
        columns = pl.ds(pl.multiple_of((first_device ^ core) * width, 128), width)
        delta = product(low, up_ref[:, columns])
        ref[core * CAP : (core + 1) * CAP, :] = delta.astype(jnp.bfloat16)


def low_kernel(scale_ref, me_ref, pick_ref, down_ref, up_ref, *refs):
    chunk_refs, (out_ref, low_ref, x_ref) = refs[:-3], refs[-3:]
    count = len(chunk_refs)
    join(range(count // 2), chunk_refs, x_ref)
    low = (product(x_ref[...], down_ref[...]) * scale_ref[0]).astype(jnp.bfloat16)
    low = product(pick_ref[...], low).astype(jnp.bfloat16)
    low_ref[...] = low
    write_deltas(low, up_ref, me_ref[0] ^ (count // 2), out_ref)


def make_low(chunks, down, up, scale, pick, me):
    count = len(chunks)
    width = up.shape[1] // count
    each, depth = chunks[0].shape
    rows = count * each
    return pl.pallas_call(
        low_kernel,
        out_shape=(
            jax.ShapeDtypeStruct((2 * CAP, width), jnp.bfloat16),
            jax.ShapeDtypeStruct((CAP, up.shape[0]), jnp.bfloat16),
            jax.ShapeDtypeStruct((rows, depth), jnp.bfloat16),
        ),
        in_specs=[SMEM, SMEM] + [VMEM] * (count + 3),
        out_specs=(VMEM,) * 3,
        compiler_params=pltpu.CompilerParams(vmem_limit_bytes=24 * MIB),
        cost_estimate=pl.CostEstimate(
            flops=2 * depth * rows * 64,
            bytes_accessed=2 * (depth * rows + down.size + up.size),
            transcendentals=0,
        ),
        name="low",
    )(scale, me, pick, down, up, *chunks)


def delta_kernel(chips, me_ref, low_ref, up_ref, *out_refs):
    for i, ref in zip(chips, out_refs):
        write_deltas(low_ref[...], up_ref, me_ref[0] ^ (2 * i), ref)


def make_deltas(low, up, me, chips, width):
    return pl.pallas_call(
        functools.partial(delta_kernel, chips),
        out_shape=tuple(jax.ShapeDtypeStruct((2 * CAP, width), jnp.bfloat16) for _ in chips),
        in_specs=[SMEM, VMEM, VMEM],
        out_specs=(VMEM,) * len(chips),
        compiler_params=pltpu.CompilerParams(vmem_limit_bytes=24 * MIB),
        cost_estimate=pl.CostEstimate(
            flops=2 * 16 * up.size, bytes_accessed=2 * up.size, transcendentals=0
        ),
        name="corrections",
    )(me, low, up)


def base_kernel(me_ref, ids_ref, x_ref, weight_ref, out_ref, place_ref, acc):
    depth, width = weight_ref.shape
    size = min(STEP, depth)
    rows, slots = place_ref.shape
    count = slots // CAP
    place_ref[...] = places_of(ids_ref[...], me_ref[0], count, slots).T
    acc[...] = jnp.zeros_like(acc)

    def step(index, block_ref):
        columns = pl.ds(pl.multiple_of(index.index[0] * size, size), size)
        acc[...] += product(x_ref[:, columns], block_ref[...])

    pltpu.emit_pipeline(
        step,
        grid=(depth // size,),
        in_specs=[pl.BlockSpec((size, width), lambda k: (k, 0), pipeline_mode=pl.Buffered(3))],
        _explicit_indices=True,
    )(weight_ref)
    each = rows // count
    for m in range(count):
        at = pl.multiple_of((me_ref[0] ^ m) * each, each)
        out_ref[pl.ds(at, each), :] = acc[m * each : (m + 1) * each, :]


def base_product(x, weight, ids, me, count):
    rows, depth = x.shape
    width = weight.shape[1]
    slots = count * CAP
    return pl.pallas_call(
        base_kernel,
        out_shape=(
            jax.ShapeDtypeStruct((rows, width), jnp.float32),
            jax.ShapeDtypeStruct((rows, slots), jnp.bfloat16),
        ),
        in_specs=[SMEM, VMEM, VMEM, HBM],
        out_specs=(VMEM, VMEM),
        scratch_shapes=[pltpu.VMEM((rows, width), jnp.float32)],
        compiler_params=pltpu.CompilerParams(vmem_limit_bytes=24 * MIB),
        cost_estimate=pl.CostEstimate(
            flops=2 * rows * depth * width, bytes_accessed=2 * weight.size, transcendentals=0
        ),
        name="base",
    )(me, ids, x, weight)


def combine_kernel(place_ref, base_ref, mate_ref, *refs):
    arrived_refs, (out_hbm, out_ref, slots, sem) = refs[:-4], refs[-4:]
    chips = len(arrived_refs)
    width = out_ref.shape[2]
    for i, ref in enumerate(arrived_refs):
        slots[i * CAP : (i + 1) * CAP, :] = ref[:CAP, :]
    half = chips * CAP
    slots[half:, :] = mate_ref[...]
    copies = []
    for i in range(out_ref.shape[0]):
        columns = pl.ds(i * width, width)
        delta = product(place_ref[...], slots[:, columns])
        out_ref[i] = (base_ref[:, columns] + delta).astype(jnp.bfloat16)
        copies.append(pltpu.make_async_copy(out_ref.at[i], out_hbm.at[:, columns], sem.at[i]))
        copies[-1].start()
    for copy in copies:
        copy.wait()


def combine(base, arrived, mate, place):
    rows, width = base.shape
    parts = 2 if width % 256 == 0 else 1
    return pl.pallas_call(
        combine_kernel,
        out_shape=jax.ShapeDtypeStruct((rows, width), jnp.bfloat16),
        in_specs=[VMEM] * (3 + len(arrived)),
        out_specs=HBM,
        scratch_shapes=[
            pltpu.VMEM((parts, rows, width // parts), jnp.bfloat16),
            pltpu.VMEM((place.shape[1], width), jnp.bfloat16),
            pltpu.SemaphoreType.DMA((parts,)),
        ],
        compiler_params=pltpu.CompilerParams(vmem_limit_bytes=24 * MIB),
        cost_estimate=pl.CostEstimate(
            flops=2 * rows * place.size, bytes_accessed=4 * base.size, transcendentals=0
        ),
        name="combine",
    )(place, base, mate, *arrived)


def plain_body(chunks, up_weight, down, up, scale, ids, me):
    count = len(chunks)
    rows, width = ids.shape[1], up_weight.shape[1]
    x = jnp.concatenate(chunks, axis=0)
    low = lax.dot_general(x, down, (((1,), (1,)), ((), ())), preferred_element_type=jnp.float32)
    pick = picks_of(ids, me[0], me[0], count)
    low = product(pick, (low * scale[0]).astype(jnp.bfloat16)).astype(jnp.bfloat16)
    delta = product(low, up).astype(jnp.bfloat16).reshape(CAP, count, width)
    arrived = lax.all_to_all(delta, AXIS, split_axis=1, concat_axis=0, tiled=True)
    base = product(x, up_weight)[origins(me[0], count, rows)[0]]
    slot = (ids * CAP + ranks(ids, count))[0]
    return (base + arrived.reshape(count * CAP, width)[slot].astype(jnp.float32)).astype(jnp.bfloat16)


def body(count, tokens, up_weight, down, up, scale, row_index):
    me = lax.axis_index(AXIS).astype(jnp.int32)[None]
    ids = row_index.reshape(1, -1)
    down, up = jnp.swapaxes(down[0], 0, 1), up[0]
    if up_weight.shape[1] % 128:
        chunks = gather_rows(tokens, count)
        return plain_body(chunks, up_weight, down, up, scale, ids, me)
    pick, down = make_plan(ids, down, me, count)
    chunks = gather_rows(tokens, count, (pick,))
    across = count // 4
    arrived = {}
    out, low, x = make_low(chunks, down, up, scale, pick, me)
    arrived[across] = swap(out, 2 * across, count)
    order = start_order(count // 2)
    others = [0] + [i for i in order if i != across]
    deltas = dict(zip(others, make_deltas(low, up, me, others, up_weight.shape[1])))
    arrived[0] = deltas[0]
    for i in others[1:]:
        arrived[i] = swap(deltas[i], 2 * i, count)
    base, place = base_product(x, up_weight, ids, me, count)
    *held, base = lax.optimization_barrier((*(arrived[i] for i in order), base))
    arrived.update(zip(order, held))
    arrived = [arrived[i] for i in range(count // 2)]
    mate = swap(jnp.concatenate([part[CAP:] for part in arrived], axis=0), 1, count)
    return combine(base, arrived, mate, place)


def solution(mesh):
    placed = (
        P(("groups", AXIS), None),
        P(None, AXIS),
        P(AXIS, None, None),
        P(AXIS, None, None),
        P(AXIS),
        P("groups", None),
    )
    return jax.shard_map(
        functools.partial(body, mesh.shape[AXIS]),
        mesh=mesh,
        in_specs=placed,
        out_specs=P("groups", AXIS),
        check_vma=False,
    )
```
